32 devices in a mesh: grp: 4 (over z), dev: 8 (over y, x, core).
Axes of the slice: x: 2, y: 2, z: 4, core: 2. Of those that a mesh axis runs over, the one named last changes fastest.
Arguments:
- pool: bfloat16 [98304, 1024], P(('grp', 'dev'))
- nearest: float32 [98304], P(('grp', 'dev')), may hold values from 0.5 to 2.2
- center_owner: int32 [4, 256], P('grp'), may hold values from 0 to 7, as said below
- center_offset: int32 [4, 256], P('grp'), may hold values from 0 to 3071
Outputs:
- nearest_after: float32 [98304], P(('grp', 'dev'))
The draws below stay inside these ranges and needn't reach their ends.
Inputs may be any that keep to these rules, and one draw needn't show every extreme that they name: `center_owner`: in each group no more than 32 centers have the same owner, one owner has exactly 32, and the centers of a group are distinct rows.
All inputs are finite; a program needn't handle non-finite values.
Results may differ from the reference program's by a relative error of at most 0.0003.
Values may be sent and summed in bfloat16 or wider, within the bound.
A program may use at most 64 MiB of HBM per device.

```python
import math
import jax
import jax.numpy as jnp
from jax import lax

D = 1024
C = 256
MOST = 32
ROWS_DEV = 3072
GROUPS = 4
POOL = 98304
N_DEV = 8


def centers_group(key):
    k_hot = jax.random.fold_in(key, 1)
    k_perm = jax.random.fold_in(key, 2)
    k_order = jax.random.fold_in(key, 3)
    k_start = jax.random.fold_in(key, 4)
    k_jitter = jax.random.fold_in(key, 5)
    hot = jax.random.randint(k_hot, (), 0, N_DEV)
    chosen = jax.random.permutation(k_perm, (N_DEV - 1) * MOST)[:C - MOST]
    other_owner = chosen // MOST
    other_owner = other_owner + (other_owner >= hot).astype(jnp.int32)
    other_rank = chosen % MOST
    owner = jnp.concatenate([jnp.full((MOST,), hot, jnp.int32), other_owner.astype(jnp.int32)])
    slot_rank = jnp.concatenate([jnp.arange(MOST, dtype=jnp.int32), other_rank.astype(jnp.int32)])
    order = jax.random.permutation(k_order, C)
    owner = owner[order]
    slot_rank = slot_rank[order]
    stride = ROWS_DEV // MOST
    starts = jax.random.randint(k_start, (N_DEV,), 0, ROWS_DEV)
    starts = jnp.where(jnp.arange(N_DEV, dtype=jnp.int32) == hot, 0, starts)
    jitter = jax.random.randint(k_jitter, (C,), 0, stride)
    is_hot = owner == hot
    jitter = jnp.where(is_hot & (slot_rank == MOST - 1), stride - 1, jitter)
    jitter = jnp.where(is_hot & (slot_rank == 0), 0, jitter)
    offset = (starts[owner] + slot_rank * stride + jitter) % ROWS_DEV
    return (owner.astype(jnp.int32), offset.astype(jnp.int32))


def centers_all(key):
    base = jax.random.fold_in(key, 4242)
    group_keys = jax.random.split(base, GROUPS)
    return jax.vmap(centers_group)(group_keys)


def draw_center_owner(key, part):
    return centers_all(key)[0]


def draw_center_offset(key, part):
    return centers_all(key)[1]


def draw_pool(key, part):
    k_proto = jax.random.fold_in(key, 11)
    k_ident = jax.random.fold_in(key, 12)
    k_noise = jax.random.fold_in(key, 13)
    protos = jax.random.normal(k_proto, (2 * C, D), jnp.float32)
    ident = jax.random.randint(k_ident, (POOL,), 0, 2 * C)
    noise = jax.random.normal(k_noise, (POOL, D), jnp.float32)
    values = (0.8 * protos[ident] + 0.6 * noise) / jnp.sqrt(jnp.float32(D))
    return values.astype(jnp.bfloat16)


def block_levels(rng, shape, pieces, smallest, largest):
    loudness = 1.0
    for dim, blocks in pieces:
        draws = jax.random.uniform(jax.random.fold_in(jax.random.fold_in(rng, 6), dim), (blocks,), jnp.float32, smallest / len(pieces), largest / len(pieces))
        loudness = loudness * jnp.repeat(jnp.exp(draws), shape[dim] // blocks).reshape((-1,) + (1,) * (len(shape) - 1 - dim))
    return loudness


def setup_inputs(seed: int = 0) -> dict:
    splits = jax.random.split(jax.random.key(seed), 5)
    pool = draw_pool(jax.random.fold_in(splits[4], 71), 0)
    nearest = jnp.clip(0.5 + 1.7 * jax.random.uniform(splits[1], (POOL,), jnp.float32) ** block_levels(splits[1], (POOL,), ((0, 32),), -0.2, 0.2), 0.5, 2.2)
    center_owner = draw_center_owner(jax.random.fold_in(splits[4], 71), 0)
    center_offset = draw_center_offset(jax.random.fold_in(splits[4], 71), 0)
    return dict(pool=pool, nearest=nearest, center_owner=center_owner, center_offset=center_offset)


def reference(pool, nearest, center_owner, center_offset):
    group_base = (jnp.arange(GROUPS, dtype=jnp.int32) * (N_DEV * ROWS_DEV))[:, None]
    index = (group_base + center_owner * ROWS_DEV + center_offset).reshape(-1).astype(jnp.int32)
    union = jnp.take(pool, index, axis=0)
    wide_union = union.astype(jnp.float32)
    center_norm = jnp.sum(wide_union * wide_union, axis=1)
    block = math.gcd(ROWS_DEV, 512)
    blocks = POOL // block

    def one_block(args):
        block_rows, block_near = args
        wide_rows = block_rows.astype(jnp.float32)
        row_norm = jnp.sum(wide_rows * wide_rows, axis=1)
        inner = jnp.dot(block_rows, union.T, preferred_element_type=jnp.float32)
        distance = jnp.maximum(row_norm[:, None] + center_norm[None, :] - 2.0 * inner, 0.0)
        return jnp.minimum(block_near, jnp.min(distance, axis=1))

    result = lax.map(one_block, (pool.reshape(blocks, block, D), nearest.reshape(blocks, block)))
    return result.reshape(POOL)
```

```python
import functools
import math

import jax
import jax.numpy as jnp
from jax import lax
from jax.experimental import pallas as pl
from jax.experimental.pallas import tpu as pltpu
from jax.sharding import PartitionSpec as P

MOST = 32
LANES = 128
MESH = pl.DeviceIdType.MESH
F32 = jnp.float32
NT = (((1,), (1,)), ((), ()))


def fused_kernel(
    owner_ref, offset_ref, nearest_ref, pool_hbm, out_ref,
    pool, union, picked, row_norm, half_norm, low,
    pool_sem, z_s, z_r, x_s, x_r, y_s, y_r, dx_s, dx_r, dy_s, dy_r, c_s, c_r,
):
    rows, width = pool.shape
    chunk = 256
    chunks = rows // chunk
    half = MOST // 2

    z = lax.axis_index("grp")
    dev = lax.axis_index("dev")
    core = dev % 2
    x = (dev // 2) % 2
    y = dev // 4
    chip = dev // 2
    x_dev = (y * 2 + (1 - x)) * 2 + core
    y_dev = ((1 - y) * 2 + x) * 2 + core
    c_dev = chip * 2 + (1 - core)
    x_chip = y * 2 + (1 - x)
    y_chip = (1 - y) * 2 + x
    d_chip = (1 - y) * 2 + (1 - x)
    layers = [z, z + 1 - 2 * (z % 2), (z + 2) % 4, 3 - z]

    barrier = pltpu.get_barrier_semaphore()
    peers = [(z, x_dev), (z, y_dev), (z, c_dev)] + [(l, dev) for l in layers[1:]]
    for peer in peers:
        pl.semaphore_signal(barrier, inc=1, device_id=peer, device_id_type=MESH)

    loads = [
        pltpu.make_async_copy(
            pool_hbm.at[pl.ds(c * chunk, chunk)], pool.at[pl.ds(c * chunk, chunk)], pool_sem.at[c]
        )
        for c in range(chunks)
    ]
    for load in loads:
        load.start()

    count = owner_ref.shape[1]
    hot = owner_ref[...] == dev
    hot_f = jnp.where(hot, 1.0, 0.0).astype(F32)
    before = lax.broadcasted_iota(jnp.int32, (count, count), 0) < lax.broadcasted_iota(
        jnp.int32, (count, count), 1
    )
    rank = jnp.dot(
        jnp.broadcast_to(hot_f, (8, count)).astype(jnp.bfloat16),
        jnp.where(before, 1.0, 0.0).astype(jnp.bfloat16),
        preferred_element_type=F32,
    )[0:1]
    slot = lax.broadcasted_iota(jnp.int32, (MOST, count), 0).astype(F32)
    chosen = jnp.where(slot == rank, 1.0, 0.0) * hot_f
    slot_offset = jnp.sum(chosen * offset_ref[...].astype(F32), axis=1, keepdims=True)

    column = lax.broadcasted_iota(jnp.int32, (MOST, chunk), 1).astype(F32)
    for c in range(chunks):
        loads[c].wait()
        one_hot = jnp.where(column + float(c * chunk) == slot_offset, 1.0, 0.0).astype(jnp.bfloat16)
        part = jnp.dot(one_hot, pool[pl.ds(c * chunk, chunk), :], preferred_element_type=F32)
        if c == 0:
            picked[...] = part
        else:
            picked[...] += part

    def place(layer, core_, chip_):
        return pl.multiple_of(((layer * 2 + core_) * 4 + chip_) * MOST, MOST)

    def copy(start, size, send, recv, to):
        ref = union.at[pl.ds(start, size)]
        return pltpu.make_async_remote_copy(
            src_ref=ref, dst_ref=ref, send_sem=send, recv_sem=recv, device_id=to, device_id_type=MESH
        )

    own = place(z, core, chip)
    union[pl.ds(own, MOST), :] = picked[...].astype(jnp.bfloat16)
    sent = []

    def send(*args):
        c = copy(*args)
        c.start()
        sent.append(c)

    def wait(start, size, send_sem, recv_sem, to):
        copy(start, size, send_sem, recv_sem, to).wait_recv()

    to_x, to_y, to_c = (z, x_dev), (z, y_dev), (z, c_dev)

    def spread(i):
        at = place(layers[i], core, chip)
        send(at, MOST, x_s.at[i], x_r.at[i], to_x)
        send(at, MOST, y_s.at[i], y_r.at[i], to_y)
        send(at, MOST, c_s.at[i], c_r.at[i], to_c)

    def along_z(k):
        send(own, MOST, z_s.at[k - 1], z_r.at[k - 1], (layers[k], dev))

    def from_z(k):
        wait(place(layers[k], core, chip), MOST, z_s.at[k - 1], z_r.at[k - 1], (layers[k], dev))
        spread(k)

    def relay(i):
        at = place(layers[i], core, x_chip)
        wait(at, MOST, x_s.at[i], x_r.at[i], to_x)
        send(at, half, dy_s.at[i], dy_r.at[i], to_y)
        send(at, MOST, c_s.at[4 + i], c_r.at[4 + i], to_c)
        at = place(layers[i], core, y_chip)
        wait(at, MOST, y_s.at[i], y_r.at[i], to_y)
        send(at + half, half, dx_s.at[i], dx_r.at[i], to_x)
        send(at, MOST, c_s.at[8 + i], c_r.at[8 + i], to_c)

    def finish(i):
        at = place(layers[i], core, d_chip)
        wait(at, half, dy_s.at[i], dy_r.at[i], to_y)
        wait(at + half, half, dx_s.at[i], dx_r.at[i], to_x)
        send(at, MOST, c_s.at[12 + i], c_r.at[12 + i], to_c)

    def across(i):
        for kind, chip_ in enumerate((chip, x_chip, y_chip, d_chip)):
            at = place(layers[i], 1 - core, chip_)
            wait(at, MOST, c_s.at[4 * kind + i], c_r.at[4 * kind + i], to_c)

    def squares(block):
        wide = block.astype(F32)
        total = wide[:, 0:LANES] * wide[:, 0:LANES]
        for k in range(1, width // LANES):
            piece = wide[:, k * LANES:(k + 1) * LANES]
            total += piece * piece
        return jnp.sum(total.T, axis=0, keepdims=True)

    def norms(first, last):
        @pl.loop(first, last)
        def _(b):
            block = pool[pl.ds(pl.multiple_of(b * LANES, LANES), LANES), :]
            row_norm[pl.ds(b, 1), :] = squares(block)

    step = 512
    steps = rows // step

    def fold(i):
        base = pl.multiple_of(layers[i] * 256, 256)
        for k in range(2):
            block = union[pl.ds(base + k * LANES, LANES), :]
            half_norm[0:1, k * LANES:(k + 1) * LANES] = 0.5 * squares(block)
        shift = half_norm[0:1, :]

        @pl.loop(0, steps)
        def _(b):
            at = pl.ds(pl.multiple_of(b * step, step), step)
            inner = lax.dot_general(
                pool[at, :], union[pl.ds(base, 256), :], NT, preferred_element_type=F32
            )
            gap = shift - inner
            gap = jnp.minimum(gap[:, :LANES], gap[:, LANES:])
            low[at, :] = gap if i == 0 else jnp.minimum(low[at, :], gap)

    pl.semaphore_wait(barrier, len(peers))
    blocks = rows // LANES
    spread(0)
    for k in range(1, 4):
        along_z(k)
    norms(0, blocks // 2)
    relay(0)
    from_z(1)
    norms(blocks // 2, blocks)
    finish(0)
    relay(1)
    from_z(2)
    across(0)
    fold(0)
    finish(1)
    relay(2)
    from_z(3)
    across(1)
    fold(1)
    finish(2)
    relay(3)
    across(2)
    fold(2)
    finish(3)
    across(3)
    fold(3)

    @pl.loop(0, blocks)
    def _(b):
        least = low[pl.ds(pl.multiple_of(b * LANES, LANES), LANES), :].T
        least = jnp.min(least, axis=0, keepdims=True)
        at = pl.ds(b, 1)
        distance = jnp.maximum(row_norm[at, :] + 2.0 * least, 0.0)
        out_ref[at, :] = jnp.minimum(nearest_ref[at, :], distance)

    for c in sent:
        c.wait_send()


def fused(pool, nearest, center_owner, center_offset):
    rows, width = pool.shape
    blocks = rows // LANES
    dma = pltpu.SemaphoreType.DMA
    vmem = pl.BlockSpec(memory_space=pltpu.VMEM)
    result = pl.pallas_call(
        fused_kernel,
        out_shape=jax.ShapeDtypeStruct((blocks, LANES), F32),
        in_specs=[vmem, vmem, vmem, pl.BlockSpec(memory_space=pltpu.HBM)],
        out_specs=vmem,
        scratch_shapes=[
            pltpu.VMEM((rows, width), jnp.bfloat16),
            pltpu.VMEM((1024, width), jnp.bfloat16),
            pltpu.VMEM((MOST, width), F32),
            pltpu.VMEM((blocks, LANES), F32),
            pltpu.VMEM((8, 256), F32),
            pltpu.VMEM((rows, LANES), F32),
            dma((rows // 256,)),
            dma((3,)), dma((3,)),
            dma((4,)), dma((4,)),
            dma((4,)), dma((4,)),
            dma((4,)), dma((4,)),
            dma((4,)), dma((4,)),
            dma((16,)), dma((16,)),
        ],
        compiler_params=pltpu.CompilerParams(
            collective_id=0, has_side_effects=True, vmem_limit_bytes=48 * 1024 * 1024
        ),
    )(center_owner, center_offset, nearest.reshape(blocks, LANES), pool)
    return result.reshape(rows)


def nearest_fold(pool_rows, row_norm, running, fragment):
    center_norm = jnp.einsum("cd,cd->c", fragment, fragment, preferred_element_type=F32)
    total_rows = pool_rows.shape[0]
    block = math.gcd(total_rows, 512)
    blocks = total_rows // block

    def one_block(args):
        block_rows, block_norm, block_near = args
        inner = lax.dot_general(block_rows, fragment, NT, preferred_element_type=F32)
        distance = jnp.maximum(block_norm[:, None] + center_norm[None, :] - 2.0 * inner, 0.0)
        return jnp.minimum(block_near, jnp.min(distance, axis=1))

    result = lax.map(
        one_block,
        (
            pool_rows.reshape(blocks, block, pool_rows.shape[1]),
            row_norm.reshape(blocks, block),
            running.reshape(blocks, block),
        ),
    )
    return result.reshape(total_rows)


def general(pool, nearest, center_owner, center_offset):
    owners = center_owner[0]
    offsets = center_offset[0]
    count = owners.shape[0]
    my_index = lax.axis_index("dev")
    per_device = count // lax.axis_size("dev")
    place = jnp.arange(count, dtype=jnp.int32)
    earlier = (owners[:, None] == owners[None, :]) & (place[None, :] < place[:, None])
    slot_rank = jnp.sum(earlier.astype(jnp.int32), axis=1)
    chosen = (
        (owners == my_index)[None, :]
        & (slot_rank[None, :] == jnp.arange(MOST, dtype=jnp.int32)[:, None])
    ).astype(jnp.int32)
    slot_offsets = jnp.sum(chosen * offsets[None, :], axis=1)
    slot_rows = jnp.take(pool, slot_offsets, axis=0)
    every_slot = lax.all_gather(slot_rows, "dev", axis=0, tiled=True)
    slot_index = owners * MOST + slot_rank
    mine = lax.dynamic_slice_in_dim(slot_index, my_index * per_device, per_device)
    local_centers = jnp.take(every_slot, mine, axis=0)
    row_norm = jnp.einsum("rd,rd->r", pool, pool, preferred_element_type=F32)
    return nearest_fold(
        pool, row_norm, nearest, lax.all_gather(local_centers, ("grp", "dev"), axis=0, tiled=True)
    )


def shards(pool, nearest, center_owner, center_offset):
    groups, devices = lax.axis_size("grp"), lax.axis_size("dev")
    full = center_owner.shape[1] == devices * MOST
    if groups == 4 and devices == 8 and full and pool.shape[0] % 512 == 0:
        return fused(pool, nearest, center_owner, center_offset)
    return general(pool, nearest, center_owner, center_offset)


def solution(mesh):
    in_specs = (P(("grp", "dev"), None), P(("grp", "dev")), P("grp", None), P("grp", None))
    out_specs = P(("grp", "dev"))
    return jax.shard_map(shards, mesh=mesh, in_specs=in_specs, out_specs=out_specs, check_vma=False)
```

```python
import functools
import math

import jax
import jax.numpy as jnp
from jax import lax
from jax.experimental import pallas as pl
from jax.experimental.pallas import tpu as pltpu
from jax.sharding import PartitionSpec as P

MOST = 32
LANES = 128
MESH = pl.DeviceIdType.MESH
F32 = jnp.float32
NT = (((1,), (1,)), ((), ()))


def fused_kernel(
    owner_hbm, offset_hbm, nearest_hbm, pool_hbm, out_ref,
    owner_ref, offset_ref, nearest_ref, picked,
    pool, union, row_norm, half_norm, low,
    in_sem, pool_sem, z_s, z_r, x_s, x_r, y_s, y_r, g_s, g_r, c_s, c_r,
):
    rows, width = pool.shape
    chunk = 256
    chunks = rows // chunk

    z = lax.axis_index("grp")
    dev = lax.axis_index("dev")
    core = dev % 2
    x = (dev // 2) % 2
    y = dev // 4
    chip = dev // 2
    x_dev = (y * 2 + (1 - x)) * 2 + core
    y_dev = ((1 - y) * 2 + x) * 2 + core
    c_dev = chip * 2 + (1 - core)
    x_chip = y * 2 + (1 - x)
    y_chip = (1 - y) * 2 + x
    d_chip = (1 - y) * 2 + (1 - x)
    g_dev = ((1 - y) * 2 + (1 - x)) * 2 + core
    layers = [z, z + 1 - 2 * (z % 2), (z + 2) % 4, 3 - z]

    barrier = pltpu.get_barrier_semaphore()
    peers = [(z, x_dev), (z, y_dev), (z, g_dev), (z, c_dev)] + [(l, dev) for l in layers[1:]]
    for peer in peers:
        pl.semaphore_signal(barrier, inc=1, device_id=peer, device_id_type=MESH)

    loads = [
        pltpu.make_async_copy(
            pool_hbm.at[pl.ds(c * chunk, chunk)], pool.at[pl.ds(c * chunk, chunk)], pool_sem.at[c]
        )
        for c in range(chunks)
    ]
    small = [
        pltpu.make_async_copy(owner_hbm, owner_ref, in_sem.at[0]),
        pltpu.make_async_copy(offset_hbm, offset_ref, in_sem.at[1]),
        pltpu.make_async_copy(nearest_hbm, nearest_ref, in_sem.at[2]),
    ]
    for load in small + loads:
        load.start()
    small[0].wait()
    small[1].wait()

    count = owner_ref.shape[1]
    hot = owner_ref[...] == dev
    hot_f = jnp.where(hot, 1.0, 0.0).astype(F32)
    before = lax.broadcasted_iota(jnp.int32, (count, count), 0) < lax.broadcasted_iota(
        jnp.int32, (count, count), 1
    )
    rank = jnp.dot(
        jnp.broadcast_to(hot_f, (8, count)).astype(jnp.bfloat16),
        jnp.where(before, 1.0, 0.0).astype(jnp.bfloat16),
        preferred_element_type=F32,
    )[0:1]
    slot = lax.broadcasted_iota(jnp.int32, (MOST, count), 0).astype(F32)
    chosen = jnp.where(slot == rank, 1.0, 0.0) * hot_f
    slot_offset = jnp.sum(chosen * offset_ref[...].astype(F32), axis=1, keepdims=True)

    column = lax.broadcasted_iota(jnp.int32, (MOST, chunk), 1).astype(F32)
    for c in range(chunks):
        loads[c].wait()
        one_hot = jnp.where(column + float(c * chunk) == slot_offset, 1.0, 0.0).astype(jnp.bfloat16)
        part = jnp.dot(one_hot, pool[pl.ds(c * chunk, chunk), :], preferred_element_type=F32)
        if c == 0:
            picked[...] = part
        else:
            picked[...] += part

    def place(layer, core_, chip_):
        return pl.multiple_of(((layer * 2 + core_) * 4 + chip_) * MOST, MOST)

    def copy(start, size, send, recv, to):
        ref = union.at[pl.ds(start, size)]
        return pltpu.make_async_remote_copy(
            src_ref=ref, dst_ref=ref, send_sem=send, recv_sem=recv, device_id=to, device_id_type=MESH
        )

    own = place(z, core, chip)
    union[pl.ds(own, MOST), :] = picked[...].astype(jnp.bfloat16)
    sent = []

    def send(*args):
        c = copy(*args)
        c.start()
        sent.append(c)

    def wait(start, size, send_sem, recv_sem, to):
        copy(start, size, send_sem, recv_sem, to).wait_recv()

    to_x, to_y, to_g, to_c = (z, x_dev), (z, y_dev), (z, g_dev), (z, c_dev)

    def spread(i):
        at = place(layers[i], core, chip)
        send(at, MOST, x_s.at[i], x_r.at[i], to_x)
        send(at, MOST, y_s.at[i], y_r.at[i], to_y)
        send(at, MOST, g_s.at[i], g_r.at[i], to_g)
        send(at, MOST, c_s.at[i], c_r.at[i], to_c)

    def along_z(k):
        send(own, MOST, z_s.at[k - 1], z_r.at[k - 1], (layers[k], dev))

    def from_z(k):
        wait(place(layers[k], core, chip), MOST, z_s.at[k - 1], z_r.at[k - 1], (layers[k], dev))
        spread(k)

    def gather(i):
        at = place(layers[i], core, x_chip)
        wait(at, MOST, x_s.at[i], x_r.at[i], to_x)
        send(at, MOST, c_s.at[4 + i], c_r.at[4 + i], to_c)
        at = place(layers[i], core, y_chip)
        wait(at, MOST, y_s.at[i], y_r.at[i], to_y)
        send(at, MOST, c_s.at[8 + i], c_r.at[8 + i], to_c)
        at = place(layers[i], core, d_chip)
        wait(at, MOST, g_s.at[i], g_r.at[i], to_g)
        send(at, MOST, c_s.at[12 + i], c_r.at[12 + i], to_c)

    def across(i):
        for kind, chip_ in enumerate((chip, x_chip, y_chip, d_chip)):
            at = place(layers[i], 1 - core, chip_)
            wait(at, MOST, c_s.at[4 * kind + i], c_r.at[4 * kind + i], to_c)

    def squares(block):
        wide = block.astype(F32)
        total = wide[:, 0:LANES] * wide[:, 0:LANES]
        for k in range(1, width // LANES):
            piece = wide[:, k * LANES:(k + 1) * LANES]
            total += piece * piece
        return jnp.sum(total.T, axis=0, keepdims=True)

    def norms(first, last):
        @pl.loop(first, last, unroll=4)
        def _(b):
            block = pool[pl.ds(pl.multiple_of(b * LANES, LANES), LANES), :]
            row_norm[pl.ds(b, 1), :] = squares(block)

    step = 1536
    steps = rows // step

    def center_norms(i):
        base = pl.multiple_of(layers[i] * 256, 256)
        for k in range(2):
            block = union[pl.ds(base + k * LANES, LANES), :]
            half_norm[0:1, k * LANES:(k + 1) * LANES] = 0.5 * squares(block)

    def fold(i, first, last):
        base = pl.multiple_of(layers[i] * 256, 256)
        shift = half_norm[0:1, :]

        @pl.loop(first, last)
        def _(b):
            at = pl.ds(pl.multiple_of(b * step, step), step)
            inner = lax.dot_general(
                pool[at, :], union[pl.ds(base, 256), :], NT, preferred_element_type=F32
            )
            gap = shift - inner
            gap = jnp.minimum(gap[:, :LANES], gap[:, LANES:])
            low[at, :] = gap if i == 0 else jnp.minimum(low[at, :], gap)

    pl.semaphore_wait(barrier, len(peers))
    blocks = rows // LANES
    for k in range(1, 4):
        along_z(k)
    spread(0)
    norms(0, blocks)
    small[2].wait()
    from_z(1)
    gather(0)
    from_z(2)
    across(0)
    center_norms(0)
    fold(0, 0, steps // 2)
    from_z(3)
    fold(0, steps // 2, steps)
    gather(1)
    across(1)
    center_norms(1)
    fold(1, 0, steps // 2)
    gather(2)
    fold(1, steps // 2, steps)
    gather(3)
    across(2)
    center_norms(2)
    fold(2, 0, steps)
    across(3)
    center_norms(3)
    fold(3, 0, steps)

    @pl.loop(0, blocks, unroll=8)
    def _(b):
        least = low[pl.ds(pl.multiple_of(b * LANES, LANES), LANES), :].T
        least = jnp.min(least, axis=0, keepdims=True)
        at = pl.ds(b, 1)
        distance = jnp.maximum(row_norm[at, :] + 2.0 * least, 0.0)
        out_ref[at, :] = jnp.minimum(nearest_ref[at, :], distance)

    for c in sent:
        c.wait_send()


def fused(pool, nearest, center_owner, center_offset):
    rows, width = pool.shape
    blocks = rows // LANES
    dma = pltpu.SemaphoreType.DMA
    vmem = pl.BlockSpec(memory_space=pltpu.VMEM)
    hbm = pl.BlockSpec(memory_space=pltpu.HBM)
    result = pl.pallas_call(
        fused_kernel,
        out_shape=jax.ShapeDtypeStruct((blocks, LANES), F32),
        in_specs=[hbm, hbm, hbm, hbm],
        out_specs=vmem,
        scratch_shapes=[
            pltpu.VMEM(center_owner.shape, jnp.int32),
            pltpu.VMEM(center_offset.shape, jnp.int32),
            pltpu.VMEM((blocks, LANES), F32),
            pltpu.VMEM((MOST, width), F32),
            pltpu.VMEM((rows, width), jnp.bfloat16),
            pltpu.VMEM((1024, width), jnp.bfloat16),
            pltpu.VMEM((blocks, LANES), F32),
            pltpu.VMEM((8, 256), F32),
            pltpu.VMEM((rows, LANES), F32),
            dma((3,)),
            dma((rows // 256,)),
            dma((3,)), dma((3,)),
            dma((4,)), dma((4,)),
            dma((4,)), dma((4,)),
            dma((4,)), dma((4,)),
            dma((16,)), dma((16,)),
        ],
        compiler_params=pltpu.CompilerParams(
            collective_id=0, has_side_effects=True, vmem_limit_bytes=48 * 1024 * 1024
        ),
    )(center_owner, center_offset, nearest.reshape(blocks, LANES), pool)
    return result.reshape(rows)


def nearest_fold(pool_rows, row_norm, running, fragment):
    center_norm = jnp.einsum("cd,cd->c", fragment, fragment, preferred_element_type=F32)
    total_rows = pool_rows.shape[0]
    block = math.gcd(total_rows, 512)
    blocks = total_rows // block

    def one_block(args):
        block_rows, block_norm, block_near = args
        inner = lax.dot_general(block_rows, fragment, NT, preferred_element_type=F32)
        distance = jnp.maximum(block_norm[:, None] + center_norm[None, :] - 2.0 * inner, 0.0)
        return jnp.minimum(block_near, jnp.min(distance, axis=1))

    result = lax.map(
        one_block,
        (
            pool_rows.reshape(blocks, block, pool_rows.shape[1]),
            row_norm.reshape(blocks, block),
            running.reshape(blocks, block),
        ),
    )
    return result.reshape(total_rows)


def general(pool, nearest, center_owner, center_offset):
    owners = center_owner[0]
    offsets = center_offset[0]
    count = owners.shape[0]
    my_index = lax.axis_index("dev")
    per_device = count // lax.axis_size("dev")
    place = jnp.arange(count, dtype=jnp.int32)
    earlier = (owners[:, None] == owners[None, :]) & (place[None, :] < place[:, None])
    slot_rank = jnp.sum(earlier.astype(jnp.int32), axis=1)
    chosen = (
        (owners == my_index)[None, :]
        & (slot_rank[None, :] == jnp.arange(MOST, dtype=jnp.int32)[:, None])
    ).astype(jnp.int32)
    slot_offsets = jnp.sum(chosen * offsets[None, :], axis=1)
    slot_rows = jnp.take(pool, slot_offsets, axis=0)
    every_slot = lax.all_gather(slot_rows, "dev", axis=0, tiled=True)
    slot_index = owners * MOST + slot_rank
    mine = lax.dynamic_slice_in_dim(slot_index, my_index * per_device, per_device)
    local_centers = jnp.take(every_slot, mine, axis=0)
    row_norm = jnp.einsum("rd,rd->r", pool, pool, preferred_element_type=F32)
    return nearest_fold(
        pool, row_norm, nearest, lax.all_gather(local_centers, ("grp", "dev"), axis=0, tiled=True)
    )


def shards(pool, nearest, center_owner, center_offset):
    groups, devices = lax.axis_size("grp"), lax.axis_size("dev")
    full = center_owner.shape[1] == devices * MOST
    if groups == 4 and devices == 8 and full and pool.shape[0] % 3072 == 0:
        return fused(pool, nearest, center_owner, center_offset)
    return general(pool, nearest, center_owner, center_offset)


def solution(mesh):
    in_specs = (P(("grp", "dev"), None), P(("grp", "dev")), P("grp", None), P("grp", None))
    out_specs = P(("grp", "dev"))
    return jax.shard_map(shards, mesh=mesh, in_specs=in_specs, out_specs=out_specs, check_vma=False)
```
